32 devices in a mesh: occ: 8 (over y, x, core), vir: 4 (over z).
Axes of the slice: x: 2, y: 2, z: 4, core: 2. Of those that a mesh axis runs over, the one named last changes fastest.
Arguments:
- amplitudes: bfloat16 [8, 128, 4096], P(None, 'occ', 'vir'), may hold values from -8 to 8
- integrals: bfloat16 [8, 2048, 4096], P(None, 'occ', 'vir'), may hold values from -0.09375 to 0.09375
- occ_energy: float32 [8, 128], P(None, ('occ', 'vir')), may hold values from 0.5 to 2
- vir_energy: float32 [8, 2048], replicated, may hold values from 1 to 3
Outputs:
- amplitude_update: float32 [8, 128, 2048], P(None, ('occ', 'vir'))
The draws below stay inside these ranges and needn't reach their ends.
All inputs are finite; a program needn't handle non-finite values.
Results may differ from the reference program's by a relative error of at most 0.0003.
Values may be sent and summed in bfloat16 or wider, within the bound.
No kernel may reach another device: no remote copies, remote signals or barrier semaphores. Data moves between devices by JAX's collectives and lax.ppermute only.
A program may use at most 64 MiB of HBM per device.

```python
import jax
import jax.numpy as jnp
from jax import lax

IRREPS = 8
OP = 128
AB = 2048
CD = 4096


def steps_of(own_key, extent, pieces, low, largest):
    factor_of = 1.0
    for dim, parts in pieces:
        steps = jax.random.uniform(jax.random.fold_in(jax.random.fold_in(own_key, 6), dim), (parts,), jnp.float32, low / len(pieces), largest / len(pieces))
        factor_of = factor_of * jnp.repeat(jnp.exp(steps), extent[dim] // parts).reshape((-1,) + (1,) * (len(extent) - 1 - dim))
    return factor_of


def centred(stream_key, shape, spread, reach, cuts=(), dtype=jnp.bfloat16):
    entries = jax.random.normal(stream_key, shape, jnp.float32) * spread
    if len(cuts) > 0:
        entries = steps_of(stream_key, shape, cuts, -0.22, 0.18) * entries
    return jnp.clip(entries, min=-reach, max=reach).astype(dtype)


def setup_inputs(seed: int = 0) -> dict:
    splits = jax.random.split(jax.random.key(seed), 5)
    amplitudes = centred(splits[0], (IRREPS, OP, CD), 2.0, 8.0, ((1, 8), (2, 4)))
    integrals = centred(splits[1], (IRREPS, AB, CD), CD ** -0.5, 0.09375, ((1, 8), (2, 4)))
    occ_energy = jnp.clip(0.5 + 1.5 * jax.random.uniform(splits[2], (IRREPS, OP), jnp.float32) ** steps_of(splits[2], (IRREPS, OP), ((1, 32),), -0.2, 0.2), 0.5, 2.0)
    vir_energy = jnp.clip(jax.random.uniform(splits[3], (IRREPS, AB), jnp.float32, 1.0, 3.0), 1.0, 3.0)
    return {"amplitudes": amplitudes, "integrals": integrals, "occ_energy": occ_energy, "vir_energy": vir_energy}


def reference(amplitudes, integrals, occ_energy, vir_energy):
    def one_irrep(pair):
        amp_block, int_block = pair
        return lax.dot_general(amp_block, int_block, (((1,), (1,)), ((), ())), preferred_element_type=jnp.float32)

    ladder = lax.map(one_irrep, (amplitudes, integrals))
    return ladder / (occ_energy[:, :, None] + vir_energy[:, None, :])
```

```python
import functools

import jax
import jax.numpy as jnp
from jax import lax
from jax.experimental import pallas as pl
from jax.experimental.pallas import tpu as pltpu
from jax.sharding import PartitionSpec as P

VMEM = pl.BlockSpec(memory_space=pltpu.VMEM)
SMEM = pl.BlockSpec(memory_space=pltpu.SMEM)
PARAMS = pltpu.CompilerParams(vmem_limit_bytes=16 << 20)


def contract_kernel(blocks, place_ref, *refs):
    amp_refs, int_ref, out_ref = refs[:blocks], refs[blocks], refs[blocks + 1]
    vir = place_ref[0]
    upper = lax.broadcasted_iota(jnp.int32, (8, int_ref.shape[1]), 0) < 4

    for g in range(int_ref.shape[0]):
        rows = jnp.concatenate([a[g] for a in amp_refs], axis=0) if blocks > 1 else amp_refs[0][g]
        sums = lax.dot_general(
            rows, int_ref[g], (((1,), (1,)), ((), ())), preferred_element_type=jnp.float32
        )
        for pair in range(blocks // 2):
            for half in range(2):
                first = sums[32 * pair + 8 * half : 32 * pair + 8 * half + 8]
                second = sums[32 * pair + 16 + 8 * half : 32 * pair + 24 + 8 * half]
                low = jnp.where(upper, first, pltpu.roll(second, 4, 0))
                high = jnp.where(upper, pltpu.roll(first, 4, 0), second)
                at = pl.ds(8 * pair, 8)
                out_ref[(2 * half) ^ vir, g, at, :] = low
                out_ref[(2 * half + 1) ^ vir, g, at, :] = high


def contract(place, pieces, integrals):
    irreps, width = integrals.shape[0], integrals.shape[1]
    rows = 4 * len(pieces)
    depth = integrals.shape[2]
    return pl.pallas_call(
        functools.partial(contract_kernel, len(pieces)),
        out_shape=jax.ShapeDtypeStruct((4, irreps, rows, width), jnp.float32),
        in_specs=[SMEM] + [VMEM] * (len(pieces) + 1),
        out_specs=VMEM,
        compiler_params=PARAMS,
        cost_estimate=pl.CostEstimate(
            flops=2 * irreps * 4 * rows * depth * width,
            bytes_accessed=2 * irreps * depth * (width + 4 * rows) + 16 * irreps * rows * width,
            transcendentals=0,
        ),
    )(place, *pieces, integrals)


def update_kernel(masks, place_ref, occ_ref, vir_ref, *refs):
    out_ref = refs[len(masks)]
    width = refs[0].shape[2]
    share = out_ref.shape[1]
    for mask, piece in zip(masks, refs):
        at = pl.ds(pl.multiple_of((place_ref[1] ^ mask) * width, width), width)
        for g in range(out_ref.shape[0]):
            levels = occ_ref[g][:, None] + vir_ref[g, at][None, :]
            out_ref[g, :, at] = piece[g] / levels


def update(place, occ_energy, vir_energy, masks, pieces):
    irreps, share = occ_energy.shape
    return pl.pallas_call(
        functools.partial(update_kernel, masks),
        out_shape=jax.ShapeDtypeStruct((irreps, share, vir_energy.shape[1]), jnp.float32),
        in_specs=[SMEM] + [VMEM] * (2 + len(pieces)),
        out_specs=VMEM,
        compiler_params=PARAMS,
    )(place, occ_energy, vir_energy, *pieces)


def swap(x, axis, mask):
    return lax.ppermute(x, axis, [(i, i ^ mask) for i in range(lax.axis_size(axis))])


def paired(groups, amplitudes, integrals, occ_energy, vir_energy):
    place = jnp.stack([lax.axis_index("vir"), lax.axis_index("occ")]).astype(jnp.int32)
    held = {0: amplitudes, 1: swap(amplitudes, "occ", 1)}
    for mask in (2, 4, 6):
        held[mask] = swap(amplitudes, "occ", mask)
        held[mask + 1] = swap(held[mask], "occ", 1)
    done = {}
    for group in groups:
        sums = contract(place, [held[m] for m in group], integrals)
        total = sums[0]
        for j in range(1, 4):
            total = total + swap(sums[j].astype(jnp.float16), "vir", j).astype(jnp.float32)
        for n, m in enumerate(group):
            part = total[:, 4 * n : 4 * n + 4]
            done[m] = swap(part, "occ", m) if m else part
    masks = sorted(done)
    return update(place, occ_energy, vir_energy, masks, [done[m] for m in masks])


def plain(amplitudes, integrals, occ_energy, vir_energy):
    n_occ = lax.axis_size("occ")
    n_vir = lax.axis_size("vir")
    irreps, rows_dev = amplitudes.shape[:2]
    share = rows_dev // n_vir
    held = lax.all_gather(amplitudes, "occ", axis=1, tiled=True)
    ladder = jnp.einsum("gic,gac->gia", held, integrals, preferred_element_type=jnp.float32)
    partial_cols = lax.psum_scatter(ladder, "vir", scatter_dimension=2, tiled=True)
    width = partial_cols.shape[2]
    moved = lax.all_to_all(partial_cols, "occ", split_axis=1, concat_axis=2, tiled=True)
    moved = lax.all_to_all(moved, "vir", split_axis=1, concat_axis=2, tiled=True)
    moved = moved.reshape(irreps, share, n_vir, n_occ, width)
    moved = jnp.transpose(moved, (0, 1, 3, 2, 4)).reshape(irreps, share, n_occ * n_vir * width)
    return moved / (occ_energy[:, :, None] + vir_energy[:, None, :])


def local(amplitudes, integrals, occ_energy, vir_energy):
    fits = lax.axis_size("occ") == 8 and lax.axis_size("vir") == 4 and amplitudes.shape[1] == 16
    if not fits:
        return plain(amplitudes, integrals, occ_energy, vir_energy)
    groups = [(0, 1, 2, 3, 4, 5, 6, 7)]
    return paired(groups, amplitudes, integrals, occ_energy, vir_energy)


def solution(mesh):
    placed = (P(None, "occ", "vir"), P(None, "occ", "vir"), P(None, ("occ", "vir")), P())
    return jax.shard_map(
        local, mesh=mesh, in_specs=placed, out_specs=P(None, ("occ", "vir"), None), check_vma=False
    )
```

```python
import functools

import jax
import jax.numpy as jnp
from jax import lax
from jax.experimental import pallas as pl
from jax.experimental.pallas import tpu as pltpu
from jax.sharding import PartitionSpec as P

VMEM = pl.BlockSpec(memory_space=pltpu.VMEM)
SMEM = pl.BlockSpec(memory_space=pltpu.SMEM)
SCALE = 64.0
MARK = jax.ShapeDtypeStruct((8, 128), jnp.float32)
PARAMS = pltpu.CompilerParams(vmem_limit_bytes=16 << 20)


def load_kernel(int_ref, slab_ref, mark_ref, sems):
    copies = [pltpu.make_async_copy(int_ref.at[g], slab_ref.at[g], sems.at[g]) for g in range(int_ref.shape[0])]
    for copy in copies:
        copy.start()
    for copy in copies:
        copy.wait()
    mark_ref[...] = jnp.zeros_like(mark_ref)


def load(integrals):
    return pl.pallas_call(
        load_kernel,
        out_shape=(jax.ShapeDtypeStruct(integrals.shape, integrals.dtype), MARK),
        in_specs=[pl.BlockSpec(memory_space=pl.ANY)],
        out_specs=(VMEM, VMEM),
        scratch_shapes=[pltpu.SemaphoreType.DMA((integrals.shape[0],))],
        compiler_params=PARAMS,
        cost_estimate=pl.CostEstimate(flops=0, bytes_accessed=4 * integrals.size, transcendentals=0),
    )(pltpu.with_memory_space_constraint(integrals, pltpu.HBM))


def contract_kernel(blocks, place_ref, seen_ref, *refs):
    amp_refs, int_ref, out_ref, mark_ref = refs[:blocks], refs[blocks], refs[blocks + 1], refs[blocks + 2]
    mark_ref[...] = jnp.zeros_like(mark_ref)
    vir = place_ref[0]
    upper = lax.broadcasted_iota(jnp.int32, (8, int_ref.shape[1]), 0) < 4
    for g in range(int_ref.shape[0]):
        rows = jnp.concatenate([a[g] for a in amp_refs], axis=0)
        sums = lax.dot_general(
            rows, int_ref[g], (((1,), (1,)), ((), ())), preferred_element_type=jnp.float32
        )
        for pair in range(blocks // 2):
            for half in range(2):
                low = sums[32 * pair + 8 * half : 32 * pair + 8 * half + 8]
                high = sums[32 * pair + 16 + 8 * half : 32 * pair + 24 + 8 * half]
                at = pl.ds(8 * pair, 8)
                out_ref[(2 * half) ^ vir, g, at, :] = jnp.where(upper, low, pltpu.roll(high, 4, 0))
                out_ref[(2 * half + 1) ^ vir, g, at, :] = jnp.where(upper, pltpu.roll(low, 4, 0), high)


def contract(place, seen, pieces, integrals):
    irreps, width, depth = integrals.shape
    rows = 4 * len(pieces)
    return pl.pallas_call(
        functools.partial(contract_kernel, len(pieces)),
        out_shape=(jax.ShapeDtypeStruct((4, irreps, rows, width), jnp.float32), MARK),
        in_specs=[SMEM] + [VMEM] * (len(pieces) + 2),
        out_specs=(VMEM, VMEM),
        compiler_params=PARAMS,
        cost_estimate=pl.CostEstimate(
            flops=2 * irreps * 4 * rows * depth * width,
            bytes_accessed=2 * irreps * depth * (width + 4 * rows) + 16 * irreps * rows * width,
            transcendentals=0,
        ),
    )(place, seen, *pieces, integrals)


def update_kernel(masks, place_ref, seen_ref, occ_ref, vir_ref, *refs):
    out_ref = refs[-1]
    width = refs[0].shape[2]
    share = out_ref.shape[1]
    for (mask, n, first), _ in zip(masks, range(len(masks))):
        piece = refs[n]
        at = pl.ds(pl.multiple_of((place_ref[1] ^ mask) * width, width), width)
        for g in range(out_ref.shape[0]):
            levels = occ_ref[g][:, None] + vir_ref[g, at][None, :]
            out_ref[g, :, at] = piece[g, first : first + share, :] / levels


def update(place, seen, occ_energy, vir_energy, masks, pieces):
    irreps, share = occ_energy.shape
    return pl.pallas_call(
        functools.partial(update_kernel, masks),
        out_shape=jax.ShapeDtypeStruct((irreps, share, vir_energy.shape[1]), jnp.float32),
        in_specs=[SMEM] + [VMEM] * (3 + len(pieces)),
        out_specs=VMEM,
        compiler_params=PARAMS,
    )(place, seen, occ_energy, vir_energy, *pieces)


def swap(x, axis, mask):
    return lax.ppermute(x, axis, [(i, i ^ mask) for i in range(lax.axis_size(axis))])


def reduced(own, sums, size):
    pieces = [swap((sums[j] * SCALE).astype(jnp.float16), "vir", j) for j in range(1, size)]
    total = pieces[0].astype(jnp.float32)
    for piece in pieces[1:]:
        total = total + piece.astype(jnp.float32)
    return own + total * (1 / SCALE)


def paired(amplitudes, integrals, occ_energy, vir_energy):
    size = lax.axis_size("vir")
    place = jnp.stack([lax.axis_index("vir"), lax.axis_index("occ")]).astype(jnp.int32)
    place, amplitudes = lax.optimization_barrier((place, amplitudes))
    half = amplitudes.shape[0] // 2
    sib = swap(amplitudes, "occ", 1)
    x = swap(amplitudes, "occ", 2)
    y = swap(amplitudes, "occ", 4)
    slab, mark = load(integrals)
    source = amplitudes
    x, y, mark = lax.optimization_barrier((x, y, mark))
    d_low, d_high = swap(x[:half], "occ", 4), swap(y[half:], "occ", 2)
    x_sib, y_sib = swap(x, "occ", 1), swap(y, "occ", 1)
    sums_b, mark = contract(place, mark, [amplitudes, sib, x, x_sib, y, y_sib], slab)
    d_low, d_high, mark = lax.optimization_barrier((d_low, d_high, mark))
    d = jnp.concatenate([d_low, d_high], axis=0)
    d_sib = swap(d, "occ", 1)
    sums_c, mark = contract(place, mark, [d, d_sib], slab)
    own, mark = lax.optimization_barrier((sums_b[0], mark))
    total_b = reduced(own, sums_b, size)
    own_c = sums_c[0]
    parts_c = [swap((sums_c[j] * SCALE).astype(jnp.float16), "vir", j) for j in range(1, size)]
    b = [swap(p, "occ", k) for k, p in ((1, total_b[:, 4:8]), (2, total_b[:, 8:12]), (3, total_b[:, 12:16]), (4, total_b[:, 16:20]), (5, total_b[:, 20:24]))]
    total_c = parts_c[0].astype(jnp.float32) + parts_c[1].astype(jnp.float32) + parts_c[2].astype(jnp.float32)
    total_c = own_c + total_c * (1 / SCALE)
    b += [swap(total_c[:, :4], "occ", 6), swap(total_c[:, 4:], "occ", 7)]
    return update(place, mark, occ_energy, vir_energy, [(k, k, 0) for k in range(8)], [total_b] + b)


def plain(amplitudes, integrals, occ_energy, vir_energy):
    n_occ = lax.axis_size("occ")
    n_vir = lax.axis_size("vir")
    irreps, rows_dev = amplitudes.shape[:2]
    share = rows_dev // n_vir
    held = lax.all_gather(amplitudes, "occ", axis=1, tiled=True)
    ladder = jnp.einsum("gic,gac->gia", held, integrals, preferred_element_type=jnp.float32)
    partial_cols = lax.psum_scatter(ladder, "vir", scatter_dimension=2, tiled=True)
    width = partial_cols.shape[2]
    moved = lax.all_to_all(partial_cols, "occ", split_axis=1, concat_axis=2, tiled=True)
    moved = lax.all_to_all(moved, "vir", split_axis=1, concat_axis=2, tiled=True)
    moved = moved.reshape(irreps, share, n_vir, n_occ, width)
    moved = jnp.transpose(moved, (0, 1, 3, 2, 4)).reshape(irreps, share, n_occ * n_vir * width)
    return moved / (occ_energy[:, :, None] + vir_energy[:, None, :])


def local(amplitudes, integrals, occ_energy, vir_energy):
    fits = lax.axis_size("occ") == 8 and lax.axis_size("vir") == 4 and amplitudes.shape[1] == 16
    if not fits:
        return plain(amplitudes, integrals, occ_energy, vir_energy)
    return paired(amplitudes, integrals, occ_energy, vir_energy)


def solution(mesh):
    placed = (P(None, "occ", "vir"), P(None, "occ", "vir"), P(None, ("occ", "vir")), P())
    return jax.shard_map(
        local, mesh=mesh, in_specs=placed, out_specs=P(None, ("occ", "vir"), None), check_vma=False
    )
```

```python
import functools

import jax
import jax.numpy as jnp
from jax import lax
from jax.experimental import pallas as pl
from jax.experimental.pallas import tpu as pltpu
from jax.sharding import PartitionSpec as P

VMEM = pl.BlockSpec(memory_space=pltpu.VMEM)
SMEM = pl.BlockSpec(memory_space=pltpu.SMEM)
SCALE = 64.0
MARK = jax.ShapeDtypeStruct((8, 128), jnp.float32)
PARAMS = pltpu.CompilerParams(vmem_limit_bytes=16 << 20)


def load_kernel(int_ref, slab_ref, mark_ref, sems):
    copies = [pltpu.make_async_copy(int_ref.at[g], slab_ref.at[g], sems.at[g]) for g in range(int_ref.shape[0])]
    for copy in copies:
        copy.start()
    for copy in copies:
        copy.wait()
    mark_ref[...] = jnp.zeros_like(mark_ref)


def load(integrals):
    return pl.pallas_call(
        load_kernel,
        out_shape=(jax.ShapeDtypeStruct(integrals.shape, integrals.dtype), MARK),
        in_specs=[pl.BlockSpec(memory_space=pl.ANY)],
        out_specs=(VMEM, VMEM),
        scratch_shapes=[pltpu.SemaphoreType.DMA((integrals.shape[0],))],
        compiler_params=PARAMS,
        cost_estimate=pl.CostEstimate(flops=0, bytes_accessed=4 * integrals.size, transcendentals=0),
    )(pltpu.with_memory_space_constraint(integrals, pltpu.HBM))


def contract_kernel(parts, blocks, place_ref, seen_ref, *refs):
    amp_refs, int_ref, out_ref, mark_ref = refs[: parts * blocks], refs[-3], refs[-2], refs[-1]
    mark_ref[...] = jnp.zeros_like(mark_ref)
    vir = place_ref[0]
    upper = lax.broadcasted_iota(jnp.int32, (8, int_ref.shape[1]), 0) < 4
    irreps = int_ref.shape[0] // parts
    for g in range(int_ref.shape[0]):
        held = amp_refs[g // irreps * blocks : (g // irreps + 1) * blocks]
        rows = [a[g % irreps] for a in held]
        rows = jnp.concatenate(rows, axis=0) if blocks > 1 else rows[0]
        sums = lax.dot_general(
            rows, int_ref[g], (((1,), (1,)), ((), ())), preferred_element_type=jnp.float32
        )
        for pair in range(rows.shape[0] // 32):
            for half in range(2):
                low = sums[32 * pair + 8 * half : 32 * pair + 8 * half + 8]
                high = sums[32 * pair + 16 + 8 * half : 32 * pair + 24 + 8 * half]
                at = pl.ds(8 * pair, 8)
                out_ref[(2 * half) ^ vir, g, at, :] = jnp.where(upper, low, pltpu.roll(high, 4, 0))
                out_ref[(2 * half + 1) ^ vir, g, at, :] = jnp.where(upper, pltpu.roll(low, 4, 0), high)


def contract(place, seen, pieces, integrals, parts=1):
    irreps, width, depth = integrals.shape
    blocks = len(pieces) // parts
    rows = sum(piece.shape[1] for piece in pieces[:blocks]) // 4
    return pl.pallas_call(
        functools.partial(contract_kernel, parts, blocks),
        out_shape=(jax.ShapeDtypeStruct((4, irreps, rows, width), jnp.float32), MARK),
        in_specs=[SMEM] + [VMEM] * (len(pieces) + 2),
        out_specs=(VMEM, VMEM),
        compiler_params=PARAMS,
        cost_estimate=pl.CostEstimate(
            flops=2 * irreps * 4 * rows * depth * width,
            bytes_accessed=2 * irreps * depth * (width + 4 * rows) + 16 * irreps * rows * width,
            transcendentals=0,
        ),
    )(place, seen, *pieces, integrals)


def update_kernel(masks, place_ref, seen_ref, occ_ref, vir_ref, *refs):
    out_ref = refs[-1]
    width = refs[0].shape[2]
    share = out_ref.shape[1]
    for (mask, n, first), _ in zip(masks, range(len(masks))):
        piece = refs[n]
        at = pl.ds(pl.multiple_of((place_ref[1] ^ mask) * width, width), width)
        for g in range(out_ref.shape[0]):
            levels = occ_ref[g][:, None] + vir_ref[g, at][None, :]
            out_ref[g, :, at] = piece[g, first : first + share, :] / levels


def update(place, seen, occ_energy, vir_energy, masks, pieces):
    irreps, share = occ_energy.shape
    return pl.pallas_call(
        functools.partial(update_kernel, masks),
        out_shape=jax.ShapeDtypeStruct((irreps, share, vir_energy.shape[1]), jnp.float32),
        in_specs=[SMEM] + [VMEM] * (3 + len(pieces)),
        out_specs=VMEM,
        compiler_params=PARAMS,
    )(place, seen, occ_energy, vir_energy, *pieces)


def swap(x, axis, mask):
    return lax.ppermute(x, axis, [(i, i ^ mask) for i in range(lax.axis_size(axis))])


def reduced(own, sums, size):
    pieces = [swap((sums[j] * SCALE).astype(jnp.float16), "vir", j) for j in (3, 1, 2)]
    total = pieces[0].astype(jnp.float32)
    for piece in pieces[1:]:
        total = total + piece.astype(jnp.float32)
    return own + total * (1 / SCALE)


def paired(amplitudes, integrals, occ_energy, vir_energy):
    size = lax.axis_size("vir")
    place = jnp.stack([lax.axis_index("vir"), lax.axis_index("occ")]).astype(jnp.int32)
    place, amplitudes = lax.optimization_barrier((place, amplitudes))
    half = amplitudes.shape[0] // 2
    sib = swap(amplitudes, "occ", 1)
    x = swap(amplitudes, "occ", 2)
    y = swap(amplitudes, "occ", 4)
    slab, mark = load(integrals)
    x, y, sib, mark = lax.optimization_barrier((x, y, sib, mark))
    x_sib, y_sib = swap(x, "occ", 1), swap(y, "occ", 1)
    d_low = swap(jnp.concatenate([x[:half], x_sib[:half]], axis=1), "occ", 4)
    d_high = swap(jnp.concatenate([y[half:], y_sib[half:]], axis=1), "occ", 2)
    pieces, nd = [d_low, d_high], 2
    sums_b, mark = contract(place, mark, [amplitudes, sib, x, x_sib, y, y_sib], slab)
    *pieces, mark = lax.optimization_barrier((*pieces, mark))
    sums_c, mark = contract(place, mark, pieces, slab, 2)
    own, mark = lax.optimization_barrier((sums_b[0], mark))
    total_b = reduced(own, sums_b, size)
    back_x, back_y = swap(total_b[:, 8:16], "occ", 2), swap(total_b[:, 16:], "occ", 4)
    own_c = sums_c[0]
    total_c = reduced(own_c, sums_c, size)
    back_d = swap(total_c, "occ", 6)
    odd = swap(jnp.concatenate([total_b[:, 4:8], back_x[:, 4:], back_y[:, 4:]], axis=1), "occ", 1)
    odd_d = swap(back_d[:, 4:], "occ", 1)
    masks = [(0, 0, 0), (1, 4, 0), (2, 1, 0), (3, 4, 4), (4, 2, 0), (5, 4, 8), (6, 3, 0), (7, 5, 0)]
    return update(place, mark, occ_energy, vir_energy, masks, [total_b, back_x, back_y, back_d, odd, odd_d])


def plain(amplitudes, integrals, occ_energy, vir_energy):
    n_occ = lax.axis_size("occ")
    n_vir = lax.axis_size("vir")
    irreps, rows_dev = amplitudes.shape[:2]
    share = rows_dev // n_vir
    held = lax.all_gather(amplitudes, "occ", axis=1, tiled=True)
    ladder = jnp.einsum("gic,gac->gia", held, integrals, preferred_element_type=jnp.float32)
    partial_cols = lax.psum_scatter(ladder, "vir", scatter_dimension=2, tiled=True)
    width = partial_cols.shape[2]
    moved = lax.all_to_all(partial_cols, "occ", split_axis=1, concat_axis=2, tiled=True)
    moved = lax.all_to_all(moved, "vir", split_axis=1, concat_axis=2, tiled=True)
    moved = moved.reshape(irreps, share, n_vir, n_occ, width)
    moved = jnp.transpose(moved, (0, 1, 3, 2, 4)).reshape(irreps, share, n_occ * n_vir * width)
    return moved / (occ_energy[:, :, None] + vir_energy[:, None, :])


def local(amplitudes, integrals, occ_energy, vir_energy):
    fits = lax.axis_size("occ") == 8 and lax.axis_size("vir") == 4 and amplitudes.shape[1] == 16
    if not fits:
        return plain(amplitudes, integrals, occ_energy, vir_energy)
    return paired(amplitudes, integrals, occ_energy, vir_energy)


def solution(mesh):
    placed = (P(None, "occ", "vir"), P(None, "occ", "vir"), P(None, ("occ", "vir")), P())
    return jax.shard_map(
        local, mesh=mesh, in_specs=placed, out_specs=P(None, ("occ", "vir"), None), check_vma=False
    )
```

```python
import functools

import jax
import jax.numpy as jnp
from jax import lax
from jax.experimental import pallas as pl
from jax.experimental.pallas import tpu as pltpu
from jax.sharding import PartitionSpec as P

VMEM = pl.BlockSpec(memory_space=pltpu.VMEM)
SCALE = 64.0
SUMS = 16.0
MARK = jax.ShapeDtypeStruct((8, 128), jnp.float32)
PARAMS = pltpu.CompilerParams(vmem_limit_bytes=16 << 20)


def load_kernel(int_ref, slab_ref, mark_ref, sems):
    copies = [pltpu.make_async_copy(int_ref.at[g], slab_ref.at[g], sems.at[g]) for g in range(int_ref.shape[0])]
    for copy in copies:
        copy.start()
    for copy in copies:
        copy.wait()
    mark_ref[...] = jnp.zeros_like(mark_ref)


def load(integrals):
    return pl.pallas_call(
        load_kernel,
        out_shape=(jax.ShapeDtypeStruct(integrals.shape, integrals.dtype), MARK),
        in_specs=[pl.BlockSpec(memory_space=pl.ANY)],
        out_specs=(VMEM, VMEM),
        scratch_shapes=[pltpu.SemaphoreType.DMA((integrals.shape[0],))],
        compiler_params=PARAMS,
        cost_estimate=pl.CostEstimate(flops=0, bytes_accessed=4 * integrals.size, transcendentals=0),
    )(pltpu.with_memory_space_constraint(integrals, pltpu.HBM))


def contract_kernel(groups, seen_ref, *refs):
    int_ref, out_ref, mark_ref = refs[-3:]
    mark_ref[...] = jnp.zeros_like(mark_ref)
    irreps, width = int_ref.shape[:2]
    vir = lax.axis_index("vir")
    upper = lax.broadcasted_iota(jnp.int32, (8, width), 0) < 4
    for g in range(irreps):
        held = [refs[n] for n in groups[g * len(groups) // irreps]]
        rows = jnp.concatenate([a[g % a.shape[0]] for a in held], axis=0)
        sums = lax.dot_general(
            rows, int_ref[g], (((1,), (1,)), ((), ())), preferred_element_type=jnp.float32
        )
        for pair in range(rows.shape[0] // 32):
            for half in range(2):
                low = sums[32 * pair + 8 * half : 32 * pair + 8 * half + 8]
                high = sums[32 * pair + 16 + 8 * half : 32 * pair + 24 + 8 * half]
                at = pl.ds(8 * pair, 8)
                out_ref[(2 * half) ^ vir, g, at, :] = jnp.where(upper, low, pltpu.roll(high, 4, 0))
                out_ref[(2 * half + 1) ^ vir, g, at, :] = jnp.where(upper, pltpu.roll(low, 4, 0), high)


def contract(seen, pieces, integrals, groups):
    irreps, width, depth = integrals.shape
    rows = sum(pieces[n].shape[1] for n in groups[0]) // 4
    return pl.pallas_call(
        functools.partial(contract_kernel, groups),
        out_shape=(jax.ShapeDtypeStruct((4, irreps, rows, width), jnp.float32), MARK),
        in_specs=[VMEM] * (len(pieces) + 2),
        out_specs=(VMEM, VMEM),
        compiler_params=PARAMS,
        cost_estimate=pl.CostEstimate(
            flops=2 * irreps * 4 * rows * depth * width,
            bytes_accessed=2 * irreps * depth * (width + 4 * rows) + 16 * irreps * rows * width,
            transcendentals=0,
        ),
    )(seen, *pieces, integrals)


def update_kernel(slabs, seen_ref, occ_ref, vir_ref, *refs):
    out_ref = refs[-1]
    width = refs[0].shape[2]
    share = out_ref.shape[1]
    occ = lax.axis_index("occ")
    y, x, core = occ // 4, occ // 2 % 2, occ % 2
    chips = {"own": 2 * y + x, "next": 2 * x + 1 - y, "last": 2 * (1 - x) + y, "far": 3 - 2 * y - x}
    for chip, flip, n, first in slabs:
        owner = 2 * chips[chip] + (1 - core if flip else core)
        at = pl.ds(pl.multiple_of(owner * width, width), width)
        for g in range(out_ref.shape[0]):
            levels = occ_ref[g][:, None] + vir_ref[g, at][None, :]
            out_ref[g, :, at] = refs[n][g, first : first + share, :] / levels


def update(seen, occ_energy, vir_energy, slabs, pieces):
    irreps, share = occ_energy.shape
    return pl.pallas_call(
        functools.partial(update_kernel, slabs),
        out_shape=jax.ShapeDtypeStruct((irreps, share, vir_energy.shape[1]), jnp.float32),
        in_specs=[VMEM] * (3 + len(pieces)),
        out_specs=VMEM,
        compiler_params=PARAMS,
    )(seen, occ_energy, vir_energy, *pieces)


def swap(x, axis, mask):
    return lax.ppermute(x, axis, [(i, i ^ mask) for i in range(lax.axis_size(axis))])


def turn(x, step):
    ring = (0, 1, 3, 2)
    return lax.ppermute(
        x,
        "occ",
        [(2 * ring[r] + core, 2 * ring[(r + step) % 4] + core) for r in range(4) for core in range(2)],
    )


def reduced(own, sums, order):
    pieces = [swap((sums[j] * SCALE).astype(jnp.float16), "vir", j) for j in order]
    total = pieces[0].astype(jnp.float32)
    for piece in pieces[1:]:
        total = total + piece.astype(jnp.float32)
    return own + total * (1 / SCALE)


def paired(amplitudes, integrals, occ_energy, vir_energy):
    half = amplitudes.shape[0] // 2
    sib = swap(amplitudes, "occ", 1)
    last = turn(amplitudes, 1)
    nxt = turn(amplitudes, -1)
    slab, mark = load(integrals)
    last, nxt, sib, mark = lax.optimization_barrier((last, nxt, sib, mark))
    last_sib, nxt_sib = swap(last, "occ", 1), swap(nxt, "occ", 1)
    low = turn(jnp.concatenate([last[:half], last_sib[:half]], axis=1), 1)
    high = turn(jnp.concatenate([nxt[half:], nxt_sib[half:]], axis=1), -1)
    sums_b, mark = contract(mark, [amplitudes, sib, last, last_sib, nxt, nxt_sib], slab, [(0, 1, 2, 3, 4, 5)])
    low, high, mark = lax.optimization_barrier((low, high, mark))
    sums_c, mark = contract(mark, [low, high], slab, [(0,), (1,)])
    own, mark = lax.optimization_barrier((sums_b[0], mark))
    total_b = reduced(own, sums_b, (2, 3, 1))
    from_next = turn(total_b[:, 8:16], -1)
    from_last = turn(total_b[:, 16:24], 1)
    total_c = reduced(sums_c[0], sums_c, (2, 3, 1))
    from_far = swap((total_c * SUMS).astype(jnp.float16), "occ", 6).astype(jnp.float32) * (1 / SUMS)
    odd = swap(jnp.concatenate([total_b[:, 4:8], from_next[:, 4:], from_last[:, 4:]], axis=1), "occ", 1)
    odd_far = swap(from_far[:, 4:], "occ", 1)
    slabs = [("own", 0, 0, 0), ("own", 1, 4, 0), ("next", 0, 1, 0), ("next", 1, 4, 4), ("last", 0, 2, 0), ("last", 1, 4, 8), ("far", 0, 3, 0), ("far", 1, 5, 0)]
    return update(mark, occ_energy, vir_energy, slabs, [total_b, from_next, from_last, from_far, odd, odd_far])


def plain(amplitudes, integrals, occ_energy, vir_energy):
    n_occ = lax.axis_size("occ")
    n_vir = lax.axis_size("vir")
    irreps, rows_dev = amplitudes.shape[:2]
    share = rows_dev // n_vir
    held = lax.all_gather(amplitudes, "occ", axis=1, tiled=True)
    ladder = jnp.einsum("gic,gac->gia", held, integrals, preferred_element_type=jnp.float32)
    partial_cols = lax.psum_scatter(ladder, "vir", scatter_dimension=2, tiled=True)
    width = partial_cols.shape[2]
    moved = lax.all_to_all(partial_cols, "occ", split_axis=1, concat_axis=2, tiled=True)
    moved = lax.all_to_all(moved, "vir", split_axis=1, concat_axis=2, tiled=True)
    moved = moved.reshape(irreps, share, n_vir, n_occ, width)
    moved = jnp.transpose(moved, (0, 1, 3, 2, 4)).reshape(irreps, share, n_occ * n_vir * width)
    return moved / (occ_energy[:, :, None] + vir_energy[:, None, :])


def local(amplitudes, integrals, occ_energy, vir_energy):
    fits = lax.axis_size("occ") == 8 and lax.axis_size("vir") == 4 and amplitudes.shape[1] == 16
    if not fits:
        return plain(amplitudes, integrals, occ_energy, vir_energy)
    return paired(amplitudes, integrals, occ_energy, vir_energy)


def solution(mesh):
    placed = (P(None, "occ", "vir"), P(None, "occ", "vir"), P(None, ("occ", "vir")), P())
    return jax.shard_map(
        local, mesh=mesh, in_specs=placed, out_specs=P(None, ("occ", "vir"), None), check_vma=False
    )
```

```python
import functools

import jax
import jax.numpy as jnp
from jax import lax
from jax.experimental import pallas as pl
from jax.experimental.pallas import tpu as pltpu
from jax.sharding import PartitionSpec as P

VMEM = pl.BlockSpec(memory_space=pltpu.VMEM)
SCALE = 64.0
SUMS = 16.0
MARK = jax.ShapeDtypeStruct((8, 128), jnp.float32)
PARAMS = pltpu.CompilerParams(vmem_limit_bytes=16 << 20)


def load_kernel(int_ref, slab_ref, mark_ref, sems):
    copies = [pltpu.make_async_copy(int_ref.at[g], slab_ref.at[g], sems.at[g]) for g in range(int_ref.shape[0])]
    for copy in copies:
        copy.start()
    for copy in copies:
        copy.wait()
    mark_ref[...] = jnp.zeros_like(mark_ref)


def load(integrals):
    return pl.pallas_call(
        load_kernel,
        out_shape=(jax.ShapeDtypeStruct(integrals.shape, integrals.dtype), MARK),
        in_specs=[pl.BlockSpec(memory_space=pl.ANY)],
        out_specs=(VMEM, VMEM),
        scratch_shapes=[pltpu.SemaphoreType.DMA((integrals.shape[0],))],
        compiler_params=PARAMS,
        cost_estimate=pl.CostEstimate(flops=0, bytes_accessed=4 * integrals.size, transcendentals=0),
    )(pltpu.with_memory_space_constraint(integrals, pltpu.HBM))


def contract_kernel(groups, seen_ref, *refs):
    int_ref, out_ref, mark_ref = refs[-3:]
    mark_ref[...] = jnp.zeros_like(mark_ref)
    irreps, width = int_ref.shape[:2]
    vir = lax.axis_index("vir")
    upper = lax.broadcasted_iota(jnp.int32, (8, width), 0) < 4
    for g in range(irreps):
        held = [refs[n] for n in groups[g * len(groups) // irreps]]
        rows = jnp.concatenate([a[g % a.shape[0]] for a in held], axis=0)
        sums = lax.dot_general(
            rows, int_ref[g], (((1,), (1,)), ((), ())), preferred_element_type=jnp.float32
        )
        for pair in range(rows.shape[0] // 32):
            for half in range(2):
                low = sums[32 * pair + 8 * half : 32 * pair + 8 * half + 8]
                high = sums[32 * pair + 16 + 8 * half : 32 * pair + 24 + 8 * half]
                at = pl.ds(8 * pair, 8)
                out_ref[(2 * half) ^ vir, g, at, :] = jnp.where(upper, low, pltpu.roll(high, 4, 0))
                out_ref[(2 * half + 1) ^ vir, g, at, :] = jnp.where(upper, pltpu.roll(low, 4, 0), high)


def contract(seen, pieces, integrals, groups):
    irreps, width, depth = integrals.shape
    rows = sum(pieces[n].shape[1] for n in groups[0]) // 4
    return pl.pallas_call(
        functools.partial(contract_kernel, groups),
        out_shape=(jax.ShapeDtypeStruct((4, irreps, rows, width), jnp.float32), MARK),
        in_specs=[VMEM] * (len(pieces) + 2),
        out_specs=(VMEM, VMEM),
        compiler_params=PARAMS,
        cost_estimate=pl.CostEstimate(
            flops=2 * irreps * 4 * rows * depth * width,
            bytes_accessed=2 * irreps * depth * (width + 4 * rows) + 16 * irreps * rows * width,
            transcendentals=0,
        ),
    )(seen, *pieces, integrals)


def update_kernel(slabs, seen_ref, occ_ref, vir_ref, *refs):
    out_ref = refs[-1]
    width = refs[0].shape[2]
    share = out_ref.shape[1]
    occ = lax.axis_index("occ")
    y, x, core = occ // 4, occ // 2 % 2, occ % 2
    chips = {"own": 2 * y + x, "next": 2 * x + 1 - y, "last": 2 * (1 - x) + y, "far": 3 - 2 * y - x}
    for chip, flip, n, first in slabs:
        owner = 2 * chips[chip] + (1 - core if flip else core)
        at = pl.ds(pl.multiple_of(owner * width, width), width)
        for g in range(out_ref.shape[0]):
            levels = occ_ref[g][:, None] + vir_ref[g, at][None, :]
            out_ref[g, :, at] = refs[n][g, first : first + share, :] / levels


def update(seen, occ_energy, vir_energy, slabs, pieces):
    irreps, share = occ_energy.shape
    return pl.pallas_call(
        functools.partial(update_kernel, slabs),
        out_shape=jax.ShapeDtypeStruct((irreps, share, vir_energy.shape[1]), jnp.float32),
        in_specs=[VMEM] * (3 + len(pieces)),
        out_specs=VMEM,
        compiler_params=PARAMS,
    )(seen, occ_energy, vir_energy, *pieces)


def swap(x, axis, mask):
    return lax.ppermute(x, axis, [(i, i ^ mask) for i in range(lax.axis_size(axis))])


def turn(x, step):
    ring = (0, 1, 3, 2)
    return lax.ppermute(
        x,
        "occ",
        [(2 * ring[r] + core, 2 * ring[(r + step) % 4] + core) for r in range(4) for core in range(2)],
    )


def reduced(own, sums, order):
    pieces = [swap((sums[j] * SCALE).astype(jnp.float16), "vir", j) for j in order]
    total = pieces[0].astype(jnp.float32)
    for piece in pieces[1:]:
        total = total + piece.astype(jnp.float32)
    return own + total * (1 / SCALE)


def paired(amplitudes, integrals, occ_energy, vir_energy):
    half = amplitudes.shape[0] // 2
    sib = swap(amplitudes, "occ", 1)
    last = turn(amplitudes, 1)
    nxt = turn(amplitudes, -1)
    slab, mark = load(integrals)
    last, nxt, sib, mark = lax.optimization_barrier((last, nxt, sib, mark))
    last_sib, nxt_sib = swap(last, "occ", 1), swap(nxt, "occ", 1)
    low = turn(jnp.concatenate([last[:half], last_sib[:half]], axis=1), 1)
    high = turn(jnp.concatenate([nxt[half:], nxt_sib[half:]], axis=1), -1)
    sums_b, mark = contract(mark, [amplitudes, sib, last, last_sib, nxt, nxt_sib], slab, [(0, 1, 2, 3, 4, 5)])
    low, high, mark = lax.optimization_barrier((low, high, mark))
    sums_c, mark = contract(mark, [low, high], slab, [(0,), (1,)])
    own, mark = lax.optimization_barrier((sums_b[0], mark))
    total_b = reduced(own, sums_b, (2, 1, 3))
    from_next = turn(total_b[:, 8:16], -1)
    from_last = turn(total_b[:, 16:24], 1)
    total_c = reduced(sums_c[0], sums_c, (2, 3, 1))
    from_far = swap((total_c * SUMS).astype(jnp.float16), "occ", 6).astype(jnp.float32) * (1 / SUMS)
    odd = swap(jnp.concatenate([total_b[:, 4:8], from_next[:, 4:], from_last[:, 4:]], axis=1), "occ", 1)
    odd_far = swap(from_far[:, 4:], "occ", 1)
    slabs = [("own", 0, 0, 0), ("own", 1, 4, 0), ("next", 0, 1, 0), ("next", 1, 4, 4), ("last", 0, 2, 0), ("last", 1, 4, 8), ("far", 0, 3, 0), ("far", 1, 5, 0)]
    return update(mark, occ_energy, vir_energy, slabs, [total_b, from_next, from_last, from_far, odd, odd_far])


def plain(amplitudes, integrals, occ_energy, vir_energy):
    n_occ = lax.axis_size("occ")
    n_vir = lax.axis_size("vir")
    irreps, rows_dev = amplitudes.shape[:2]
    share = rows_dev // n_vir
    held = lax.all_gather(amplitudes, "occ", axis=1, tiled=True)
    ladder = jnp.einsum("gic,gac->gia", held, integrals, preferred_element_type=jnp.float32)
    partial_cols = lax.psum_scatter(ladder, "vir", scatter_dimension=2, tiled=True)
    width = partial_cols.shape[2]
    moved = lax.all_to_all(partial_cols, "occ", split_axis=1, concat_axis=2, tiled=True)
    moved = lax.all_to_all(moved, "vir", split_axis=1, concat_axis=2, tiled=True)
    moved = moved.reshape(irreps, share, n_vir, n_occ, width)
    moved = jnp.transpose(moved, (0, 1, 3, 2, 4)).reshape(irreps, share, n_occ * n_vir * width)
    return moved / (occ_energy[:, :, None] + vir_energy[:, None, :])


def local(amplitudes, integrals, occ_energy, vir_energy):
    fits = lax.axis_size("occ") == 8 and lax.axis_size("vir") == 4 and amplitudes.shape[1] == 16
    if not fits:
        return plain(amplitudes, integrals, occ_energy, vir_energy)
    return paired(amplitudes, integrals, occ_energy, vir_energy)


def solution(mesh):
    placed = (P(None, "occ", "vir"), P(None, "occ", "vir"), P(None, ("occ", "vir")), P())
    return jax.shard_map(
        local, mesh=mesh, in_specs=placed, out_specs=P(None, ("occ", "vir"), None), check_vma=False
    )
```

```python
import functools

import jax
import jax.numpy as jnp
from jax import lax
from jax.experimental import pallas as pl
from jax.experimental.pallas import tpu as pltpu
from jax.sharding import PartitionSpec as P

VMEM = pl.BlockSpec(memory_space=pltpu.VMEM)
SCALE = 64.0
SUMS = 16.0
MARK = jax.ShapeDtypeStruct((8, 128), jnp.float32)
PARAMS = pltpu.CompilerParams(vmem_limit_bytes=16 << 20)


def load_kernel(int_ref, slab_ref, mark_ref, sems):
    copies = [pltpu.make_async_copy(int_ref.at[g], slab_ref.at[g], sems.at[g]) for g in range(int_ref.shape[0])]
    for copy in copies:
        copy.start()
    for copy in copies:
        copy.wait()
    mark_ref[...] = jnp.zeros_like(mark_ref)


def load(integrals):
    return pl.pallas_call(
        load_kernel,
        out_shape=(jax.ShapeDtypeStruct(integrals.shape, integrals.dtype), MARK),
        in_specs=[pl.BlockSpec(memory_space=pl.ANY)],
        out_specs=(VMEM, VMEM),
        scratch_shapes=[pltpu.SemaphoreType.DMA((integrals.shape[0],))],
        compiler_params=PARAMS,
        cost_estimate=pl.CostEstimate(flops=0, bytes_accessed=4 * integrals.size, transcendentals=0),
    )(pltpu.with_memory_space_constraint(integrals, pltpu.HBM))


def contract_kernel(groups, start, seen_ref, *refs):
    int_ref, out_ref, mark_ref = refs[-3:]
    mark_ref[...] = jnp.zeros_like(mark_ref)
    irreps, width = out_ref.shape[1], int_ref.shape[1]
    vir = lax.axis_index("vir")
    upper = lax.broadcasted_iota(jnp.int32, (8, width), 0) < 4
    for g in range(irreps):
        held = [refs[n] for n in groups[g * len(groups) // irreps]]
        rows = jnp.concatenate([a[g % a.shape[0]] for a in held], axis=0)
        sums = lax.dot_general(
            rows, int_ref[start + g], (((1,), (1,)), ((), ())), preferred_element_type=jnp.float32
        )
        for pair in range(rows.shape[0] // 32):
            for half in range(2):
                low = sums[32 * pair + 8 * half : 32 * pair + 8 * half + 8]
                high = sums[32 * pair + 16 + 8 * half : 32 * pair + 24 + 8 * half]
                at = pl.ds(8 * pair, 8)
                out_ref[(2 * half) ^ vir, g, at, :] = jnp.where(upper, low, pltpu.roll(high, 4, 0))
                out_ref[(2 * half + 1) ^ vir, g, at, :] = jnp.where(upper, pltpu.roll(low, 4, 0), high)


def contract(seen, pieces, integrals, groups, start=0, irreps=None):
    width, depth = integrals.shape[1:]
    irreps = irreps or integrals.shape[0]
    rows = sum(pieces[n].shape[1] for n in groups[0]) // 4
    return pl.pallas_call(
        functools.partial(contract_kernel, groups, start),
        out_shape=(jax.ShapeDtypeStruct((4, irreps, rows, width), jnp.float32), MARK),
        in_specs=[VMEM] * (len(pieces) + 2),
        out_specs=(VMEM, VMEM),
        compiler_params=PARAMS,
        cost_estimate=pl.CostEstimate(
            flops=2 * irreps * 4 * rows * depth * width,
            bytes_accessed=2 * irreps * depth * (width + 4 * rows) + 16 * irreps * rows * width,
            transcendentals=0,
        ),
    )(seen, *pieces, integrals)


def update_kernel(slabs, seen_ref, occ_ref, vir_ref, *refs):
    out_ref = refs[-1]
    width = refs[0].shape[2]
    share = out_ref.shape[1]
    occ = lax.axis_index("occ")
    y, x, core = occ // 4, occ // 2 % 2, occ % 2
    chips = {"own": 2 * y + x, "next": 2 * x + 1 - y, "last": 2 * (1 - x) + y, "far": 3 - 2 * y - x}
    for chip, flip, n, first in slabs:
        owner = 2 * chips[chip] + (1 - core if flip else core)
        at = pl.ds(pl.multiple_of(owner * width, width), width)
        for g in range(out_ref.shape[0]):
            levels = occ_ref[g][:, None] + vir_ref[g, at][None, :]
            out_ref[g, :, at] = refs[n][g, first : first + share, :] / levels


def update(seen, occ_energy, vir_energy, slabs, pieces):
    irreps, share = occ_energy.shape
    return pl.pallas_call(
        functools.partial(update_kernel, slabs),
        out_shape=jax.ShapeDtypeStruct((irreps, share, vir_energy.shape[1]), jnp.float32),
        in_specs=[VMEM] * (3 + len(pieces)),
        out_specs=VMEM,
        compiler_params=PARAMS,
    )(seen, occ_energy, vir_energy, *pieces)


def swap(x, axis, mask):
    return lax.ppermute(x, axis, [(i, i ^ mask) for i in range(lax.axis_size(axis))])


def turn(x, step):
    ring = (0, 1, 3, 2)
    return lax.ppermute(
        x,
        "occ",
        [(2 * ring[r] + core, 2 * ring[(r + step) % 4] + core) for r in range(4) for core in range(2)],
    )


def reduced(own, sums, order):
    pieces = [swap((sums[j] * SCALE).astype(jnp.float16), "vir", j) for j in order]
    total = pieces[0].astype(jnp.float32)
    for piece in pieces[1:]:
        total = total + piece.astype(jnp.float32)
    return own + total * (1 / SCALE)


def paired(amplitudes, integrals, occ_energy, vir_energy):
    half = amplitudes.shape[0] // 2
    sib = swap(amplitudes, "occ", 1)
    last = turn(amplitudes, 1)
    nxt = turn(amplitudes, -1)
    slab, mark = load(integrals)
    last, nxt, sib, mark = lax.optimization_barrier((last, nxt, sib, mark))
    last_sib, nxt_sib = swap(last, "occ", 1), swap(nxt, "occ", 1)
    low = turn(jnp.concatenate([last[:half], last_sib[:half]], axis=1), 1)
    high = turn(jnp.concatenate([nxt[half:], nxt_sib[half:]], axis=1), -1)
    sums_b, mark = contract(mark, [amplitudes, sib, last, last_sib, nxt, nxt_sib], slab, [(0, 1, 2, 3, 4, 5)])
    low, mark = lax.optimization_barrier((low, mark))
    sums_low, mark = contract(mark, [low], slab, [(0,)], 0, half)
    high, mark = lax.optimization_barrier((high, mark))
    sums_high, mark = contract(mark, [high], slab, [(0,)], half, half)
    sums_c = [jnp.concatenate([sums_low[j], sums_high[j]], axis=0) for j in range(sums_low.shape[0])]
    own, mark = lax.optimization_barrier((sums_b[0], mark))
    total_b = reduced(own, sums_b, (2, 1, 3))
    from_next = turn(total_b[:, 8:16], -1)
    from_last = turn(total_b[:, 16:24], 1)
    total_c = reduced(sums_c[0], sums_c, (2, 3, 1))
    from_far = swap((total_c * SUMS).astype(jnp.float16), "occ", 6).astype(jnp.float32) * (1 / SUMS)
    odd = swap(jnp.concatenate([total_b[:, 4:8], from_next[:, 4:], from_last[:, 4:]], axis=1), "occ", 1)
    odd_far = swap(from_far[:, 4:], "occ", 1)
    slabs = [("own", 0, 0, 0), ("own", 1, 4, 0), ("next", 0, 1, 0), ("next", 1, 4, 4), ("last", 0, 2, 0), ("last", 1, 4, 8), ("far", 0, 3, 0), ("far", 1, 5, 0)]
    return update(mark, occ_energy, vir_energy, slabs, [total_b, from_next, from_last, from_far, odd, odd_far])


def plain(amplitudes, integrals, occ_energy, vir_energy):
    n_occ = lax.axis_size("occ")
    n_vir = lax.axis_size("vir")
    irreps, rows_dev = amplitudes.shape[:2]
    share = rows_dev // n_vir
    held = lax.all_gather(amplitudes, "occ", axis=1, tiled=True)
    ladder = jnp.einsum("gic,gac->gia", held, integrals, preferred_element_type=jnp.float32)
    partial_cols = lax.psum_scatter(ladder, "vir", scatter_dimension=2, tiled=True)
    width = partial_cols.shape[2]
    moved = lax.all_to_all(partial_cols, "occ", split_axis=1, concat_axis=2, tiled=True)
    moved = lax.all_to_all(moved, "vir", split_axis=1, concat_axis=2, tiled=True)
    moved = moved.reshape(irreps, share, n_vir, n_occ, width)
    moved = jnp.transpose(moved, (0, 1, 3, 2, 4)).reshape(irreps, share, n_occ * n_vir * width)
    return moved / (occ_energy[:, :, None] + vir_energy[:, None, :])


def local(amplitudes, integrals, occ_energy, vir_energy):
    fits = lax.axis_size("occ") == 8 and lax.axis_size("vir") == 4 and amplitudes.shape[1] == 16
    if not fits:
        return plain(amplitudes, integrals, occ_energy, vir_energy)
    return paired(amplitudes, integrals, occ_energy, vir_energy)


def solution(mesh):
    placed = (P(None, "occ", "vir"), P(None, "occ", "vir"), P(None, ("occ", "vir")), P())
    return jax.shard_map(
        local, mesh=mesh, in_specs=placed, out_specs=P(None, ("occ", "vir"), None), check_vma=False
    )
```

```python
import functools

import jax
import jax.numpy as jnp
from jax import lax
from jax.experimental import pallas as pl
from jax.experimental.pallas import tpu as pltpu
from jax.sharding import PartitionSpec as P

VMEM = pl.BlockSpec(memory_space=pltpu.VMEM)
SCALE = 64.0
SUMS = 16.0
MARK = jax.ShapeDtypeStruct((8, 128), jnp.float32)
PARAMS = pltpu.CompilerParams(vmem_limit_bytes=16 << 20)


def load_kernel(int_ref, slab_ref, mark_ref, sems):
    copies = [pltpu.make_async_copy(int_ref.at[g], slab_ref.at[g], sems.at[g]) for g in range(int_ref.shape[0])]
    for copy in copies:
        copy.start()
    for copy in copies:
        copy.wait()
    mark_ref[...] = jnp.zeros_like(mark_ref)


def load(integrals):
    return pl.pallas_call(
        load_kernel,
        out_shape=(jax.ShapeDtypeStruct(integrals.shape, integrals.dtype), MARK),
        in_specs=[pl.BlockSpec(memory_space=pl.ANY)],
        out_specs=(VMEM, VMEM),
        scratch_shapes=[pltpu.SemaphoreType.DMA((integrals.shape[0],))],
        compiler_params=PARAMS,
        cost_estimate=pl.CostEstimate(flops=0, bytes_accessed=4 * integrals.size, transcendentals=0),
    )(pltpu.with_memory_space_constraint(integrals, pltpu.HBM))


def contract_kernel(groups, seen_ref, *refs):
    int_ref, out_ref, mark_ref = refs[-3:]
    mark_ref[...] = jnp.zeros_like(mark_ref)
    irreps, width = int_ref.shape[:2]
    vir = lax.axis_index("vir")
    upper = lax.broadcasted_iota(jnp.int32, (8, width), 0) < 4
    for g in range(irreps):
        held = [refs[n] for n in groups[g * len(groups) // irreps]]
        rows = jnp.concatenate([a[g % a.shape[0]] for a in held], axis=0)
        sums = lax.dot_general(
            rows, int_ref[g], (((1,), (1,)), ((), ())), preferred_element_type=jnp.float32
        )
        for pair in range(rows.shape[0] // 32):
            for half in range(2):
                low = sums[32 * pair + 8 * half : 32 * pair + 8 * half + 8]
                high = sums[32 * pair + 16 + 8 * half : 32 * pair + 24 + 8 * half]
                at = pl.ds(8 * pair, 8)
                out_ref[(2 * half) ^ vir, g, at, :] = jnp.where(upper, low, pltpu.roll(high, 4, 0))
                out_ref[(2 * half + 1) ^ vir, g, at, :] = jnp.where(upper, pltpu.roll(low, 4, 0), high)


def contract(seen, pieces, integrals, groups):
    irreps, width, depth = integrals.shape
    rows = sum(pieces[n].shape[1] for n in groups[0]) // 4
    return pl.pallas_call(
        functools.partial(contract_kernel, groups),
        out_shape=(jax.ShapeDtypeStruct((4, irreps, rows, width), jnp.float32), MARK),
        in_specs=[VMEM] * (len(pieces) + 2),
        out_specs=(VMEM, VMEM),
        compiler_params=PARAMS,
        cost_estimate=pl.CostEstimate(
            flops=2 * irreps * 4 * rows * depth * width,
            bytes_accessed=2 * irreps * depth * (width + 4 * rows) + 16 * irreps * rows * width,
            transcendentals=0,
        ),
    )(seen, *pieces, integrals)


def update_kernel(slabs, seen_ref, occ_ref, vir_ref, *refs):
    out_ref = refs[-1]
    width = refs[0].shape[2]
    share = out_ref.shape[1]
    occ = lax.axis_index("occ")
    y, x, core = occ // 4, occ // 2 % 2, occ % 2
    chips = {"own": 2 * y + x, "next": 2 * x + 1 - y, "last": 2 * (1 - x) + y, "far": 3 - 2 * y - x}
    for chip, flip, n, first in slabs:
        owner = 2 * chips[chip] + (1 - core if flip else core)
        at = pl.ds(pl.multiple_of(owner * width, width), width)
        for g in range(out_ref.shape[0]):
            levels = occ_ref[g][:, None] + vir_ref[g, at][None, :]
            out_ref[g, :, at] = refs[n][g, first : first + share, :] / levels


def update(seen, occ_energy, vir_energy, slabs, pieces):
    irreps, share = occ_energy.shape
    return pl.pallas_call(
        functools.partial(update_kernel, slabs),
        out_shape=jax.ShapeDtypeStruct((irreps, share, vir_energy.shape[1]), jnp.float32),
        in_specs=[VMEM] * (3 + len(pieces)),
        out_specs=VMEM,
        compiler_params=PARAMS,
    )(seen, occ_energy, vir_energy, *pieces)


def swap(x, axis, mask):
    return lax.ppermute(x, axis, [(i, i ^ mask) for i in range(lax.axis_size(axis))])


def turn(x, step):
    ring = (0, 1, 3, 2)
    return lax.ppermute(
        x,
        "occ",
        [(2 * ring[r] + core, 2 * ring[(r + step) % 4] + core) for r in range(4) for core in range(2)],
    )


def reduced(own, sums, order):
    pieces = [swap((sums[j] * SCALE).astype(jnp.float16), "vir", j) for j in order]
    total = pieces[0].astype(jnp.float32)
    for piece in pieces[1:]:
        total = total + piece.astype(jnp.float32)
    return own + total * (1 / SCALE)


def paired(amplitudes, integrals, occ_energy, vir_energy):
    half = amplitudes.shape[0] // 2
    sib = swap(amplitudes, "occ", 1)
    last = turn(amplitudes, 1)
    nxt = turn(amplitudes, -1)
    slab, mark = load(integrals)
    last, nxt, sib, mark = lax.optimization_barrier((last, nxt, sib, mark))
    last_sib, nxt_sib = swap(last, "occ", 1), swap(nxt, "occ", 1)
    low = turn(jnp.concatenate([last[:half], last_sib[:half]], axis=1), 1)
    high = turn(jnp.concatenate([nxt[half:], nxt_sib[half:]], axis=1), -1)
    sums_b, mark = contract(mark, [amplitudes, sib, last, last_sib, nxt, nxt_sib], slab, [(0, 1, 2, 3, 4, 5)])
    low, high, mark = lax.optimization_barrier((low, high, mark))
    sums_c, mark = contract(mark, [low, high], slab, [(0,), (1,)])
    own, mark = lax.optimization_barrier((sums_b[0], mark))
    total_b = reduced(own, sums_b, (2, 1, 3))
    from_next = turn(total_b[:, 8:16], -1)
    from_last = turn(total_b[:, 16:24], 1)
    total_c = reduced(sums_c[0], sums_c, (2, 3, 1))
    from_far = swap((total_c * SUMS).astype(jnp.float16), "occ", 6).astype(jnp.float32) * (1 / SUMS)
    odd = swap(jnp.concatenate([from_next[:, 4:], from_last[:, 4:]], axis=1), "occ", 1)
    odd_own = swap(total_b[:, 4:8], "occ", 1)
    odd_far = swap(from_far[:, 4:], "occ", 1)
    slabs = [("own", 0, 0, 0), ("own", 1, 6, 0), ("next", 0, 1, 0), ("next", 1, 4, 0), ("last", 0, 2, 0), ("last", 1, 4, 4), ("far", 0, 3, 0), ("far", 1, 5, 0)]
    return update(mark, occ_energy, vir_energy, slabs, [total_b, from_next, from_last, from_far, odd, odd_far, odd_own])


def plain(amplitudes, integrals, occ_energy, vir_energy):
    n_occ = lax.axis_size("occ")
    n_vir = lax.axis_size("vir")
    irreps, rows_dev = amplitudes.shape[:2]
    share = rows_dev // n_vir
    held = lax.all_gather(amplitudes, "occ", axis=1, tiled=True)
    ladder = jnp.einsum("gic,gac->gia", held, integrals, preferred_element_type=jnp.float32)
    partial_cols = lax.psum_scatter(ladder, "vir", scatter_dimension=2, tiled=True)
    width = partial_cols.shape[2]
    moved = lax.all_to_all(partial_cols, "occ", split_axis=1, concat_axis=2, tiled=True)
    moved = lax.all_to_all(moved, "vir", split_axis=1, concat_axis=2, tiled=True)
    moved = moved.reshape(irreps, share, n_vir, n_occ, width)
    moved = jnp.transpose(moved, (0, 1, 3, 2, 4)).reshape(irreps, share, n_occ * n_vir * width)
    return moved / (occ_energy[:, :, None] + vir_energy[:, None, :])


def local(amplitudes, integrals, occ_energy, vir_energy):
    fits = lax.axis_size("occ") == 8 and lax.axis_size("vir") == 4 and amplitudes.shape[1] == 16
    if not fits:
        return plain(amplitudes, integrals, occ_energy, vir_energy)
    return paired(amplitudes, integrals, occ_energy, vir_energy)


def solution(mesh):
    placed = (P(None, "occ", "vir"), P(None, "occ", "vir"), P(None, ("occ", "vir")), P())
    return jax.shard_map(
        local, mesh=mesh, in_specs=placed, out_specs=P(None, ("occ", "vir"), None), check_vma=False
    )
```

```python
import functools

import jax
import jax.numpy as jnp
from jax import lax
from jax.experimental import pallas as pl
from jax.experimental.pallas import tpu as pltpu
from jax.sharding import PartitionSpec as P

VMEM = pl.BlockSpec(memory_space=pltpu.VMEM)
SCALE = 64.0
SUMS = 16.0
MARK = jax.ShapeDtypeStruct((8, 128), jnp.float32)
PARAMS = pltpu.CompilerParams(vmem_limit_bytes=16 << 20)


def load_kernel(int_ref, slab_ref, mark_ref, sems):
    copies = [pltpu.make_async_copy(int_ref.at[g], slab_ref.at[g], sems.at[g]) for g in range(int_ref.shape[0])]
    for copy in copies:
        copy.start()
    for copy in copies:
        copy.wait()
    mark_ref[...] = jnp.zeros_like(mark_ref)


def load(integrals):
    return pl.pallas_call(
        load_kernel,
        out_shape=(jax.ShapeDtypeStruct(integrals.shape, integrals.dtype), MARK),
        in_specs=[pl.BlockSpec(memory_space=pl.ANY)],
        out_specs=(VMEM, VMEM),
        scratch_shapes=[pltpu.SemaphoreType.DMA((integrals.shape[0],))],
        compiler_params=PARAMS,
        cost_estimate=pl.CostEstimate(flops=0, bytes_accessed=4 * integrals.size, transcendentals=0),
    )(pltpu.with_memory_space_constraint(integrals, pltpu.HBM))


def contract_kernel(groups, seen_ref, *refs):
    int_ref, out_ref, mark_ref = refs[-3:]
    mark_ref[...] = jnp.zeros_like(mark_ref)
    irreps, width = int_ref.shape[:2]
    vir = lax.axis_index("vir")
    upper = lax.broadcasted_iota(jnp.int32, (8, width), 0) < 4
    for g in range(irreps):
        held = [refs[n] for n in groups[g * len(groups) // irreps]]
        rows = jnp.concatenate([a[g % a.shape[0]] for a in held], axis=0)
        sums = lax.dot_general(
            rows, int_ref[g], (((1,), (1,)), ((), ())), preferred_element_type=jnp.float32
        )
        for pair in range(rows.shape[0] // 32):
            for half in range(2):
                low = sums[32 * pair + 8 * half : 32 * pair + 8 * half + 8]
                high = sums[32 * pair + 16 + 8 * half : 32 * pair + 24 + 8 * half]
                at = pl.ds(8 * pair, 8)
                out_ref[(2 * half) ^ vir, g, at, :] = jnp.where(upper, low, pltpu.roll(high, 4, 0))
                out_ref[(2 * half + 1) ^ vir, g, at, :] = jnp.where(upper, pltpu.roll(low, 4, 0), high)


def contract(seen, pieces, integrals, groups):
    irreps, width, depth = integrals.shape
    rows = sum(pieces[n].shape[1] for n in groups[0]) // 4
    return pl.pallas_call(
        functools.partial(contract_kernel, groups),
        out_shape=(jax.ShapeDtypeStruct((4, irreps, rows, width), jnp.float32), MARK),
        in_specs=[VMEM] * (len(pieces) + 2),
        out_specs=(VMEM, VMEM),
        compiler_params=PARAMS,
        cost_estimate=pl.CostEstimate(
            flops=2 * irreps * 4 * rows * depth * width,
            bytes_accessed=2 * irreps * depth * (width + 4 * rows) + 16 * irreps * rows * width,
            transcendentals=0,
        ),
    )(seen, *pieces, integrals)


def update_kernel(slabs, seen_ref, occ_ref, vir_ref, *refs):
    out_ref = refs[-1]
    width = refs[0].shape[2]
    share = out_ref.shape[1]
    occ = lax.axis_index("occ")
    y, x, core = occ // 4, occ // 2 % 2, occ % 2
    chips = {"own": 2 * y + x, "next": 2 * x + 1 - y, "last": 2 * (1 - x) + y, "far": 3 - 2 * y - x}
    for chip, flip, n, first in slabs:
        owner = 2 * chips[chip] + (1 - core if flip else core)
        at = pl.ds(pl.multiple_of(owner * width, width), width)
        for g in range(out_ref.shape[0]):
            levels = occ_ref[g][:, None] + vir_ref[g, at][None, :]
            out_ref[g, :, at] = refs[n][g, first : first + share, :] / levels


def update(seen, occ_energy, vir_energy, slabs, pieces):
    irreps, share = occ_energy.shape
    return pl.pallas_call(
        functools.partial(update_kernel, slabs),
        out_shape=jax.ShapeDtypeStruct((irreps, share, vir_energy.shape[1]), jnp.float32),
        in_specs=[VMEM] * (3 + len(pieces)),
        out_specs=VMEM,
        compiler_params=PARAMS,
    )(seen, occ_energy, vir_energy, *pieces)


def swap(x, axis, mask):
    return lax.ppermute(x, axis, [(i, i ^ mask) for i in range(lax.axis_size(axis))])


def turn(x, step):
    ring = (0, 1, 3, 2)
    return lax.ppermute(
        x,
        "occ",
        [(2 * ring[r] + core, 2 * ring[(r + step) % 4] + core) for r in range(4) for core in range(2)],
    )


def reduced(own, sums, order):
    pieces = [swap((sums[j] * SCALE).astype(jnp.float16), "vir", j) for j in order]
    total = pieces[0].astype(jnp.float32)
    for piece in pieces[1:]:
        total = total + piece.astype(jnp.float32)
    return own + total * (1 / SCALE)


def paired(amplitudes, integrals, occ_energy, vir_energy):
    half = amplitudes.shape[0] // 2
    sib = swap(amplitudes, "occ", 1)
    last = turn(amplitudes, 1)
    nxt = turn(amplitudes, -1)
    slab, mark = load(integrals)
    last, nxt, sib, mark = lax.optimization_barrier((last, nxt, sib, mark))
    last_sib, nxt_sib = swap(last, "occ", 1), swap(nxt, "occ", 1)
    low = turn(jnp.concatenate([last[half:], last_sib[half:]], axis=1), 1)
    high = turn(jnp.concatenate([nxt[:half], nxt_sib[:half]], axis=1), -1)
    sums_b, mark = contract(mark, [amplitudes, sib, last, last_sib, nxt, nxt_sib], slab, [(0, 1, 2, 3, 4, 5)])
    low, high, mark = lax.optimization_barrier((low, high, mark))
    sums_c, mark = contract(mark, [high, low], slab, [(0,), (1,)])
    own, mark = lax.optimization_barrier((sums_b[0], mark))
    total_b = reduced(own, sums_b, (2, 1, 3))
    from_next = turn(total_b[:, 8:16], -1)
    from_last = turn(total_b[:, 16:24], 1)
    total_c = reduced(sums_c[0], sums_c, (2, 3, 1))
    from_far = swap((total_c * SUMS).astype(jnp.float16), "occ", 6).astype(jnp.float32) * (1 / SUMS)
    odd = swap(jnp.concatenate([total_b[:, 4:8], from_next[:, 4:], from_last[:, 4:]], axis=1), "occ", 1)
    odd_far = swap(from_far[:, 4:], "occ", 1)
    slabs = [("own", 0, 0, 0), ("own", 1, 4, 0), ("next", 0, 1, 0), ("next", 1, 4, 4), ("last", 0, 2, 0), ("last", 1, 4, 8), ("far", 0, 3, 0), ("far", 1, 5, 0)]
    return update(mark, occ_energy, vir_energy, slabs, [total_b, from_next, from_last, from_far, odd, odd_far])


def plain(amplitudes, integrals, occ_energy, vir_energy):
    n_occ = lax.axis_size("occ")
    n_vir = lax.axis_size("vir")
    irreps, rows_dev = amplitudes.shape[:2]
    share = rows_dev // n_vir
    held = lax.all_gather(amplitudes, "occ", axis=1, tiled=True)
    ladder = jnp.einsum("gic,gac->gia", held, integrals, preferred_element_type=jnp.float32)
    partial_cols = lax.psum_scatter(ladder, "vir", scatter_dimension=2, tiled=True)
    width = partial_cols.shape[2]
    moved = lax.all_to_all(partial_cols, "occ", split_axis=1, concat_axis=2, tiled=True)
    moved = lax.all_to_all(moved, "vir", split_axis=1, concat_axis=2, tiled=True)
    moved = moved.reshape(irreps, share, n_vir, n_occ, width)
    moved = jnp.transpose(moved, (0, 1, 3, 2, 4)).reshape(irreps, share, n_occ * n_vir * width)
    return moved / (occ_energy[:, :, None] + vir_energy[:, None, :])


def local(amplitudes, integrals, occ_energy, vir_energy):
    fits = lax.axis_size("occ") == 8 and lax.axis_size("vir") == 4 and amplitudes.shape[1] == 16
    if not fits:
        return plain(amplitudes, integrals, occ_energy, vir_energy)
    return paired(amplitudes, integrals, occ_energy, vir_energy)


def solution(mesh):
    placed = (P(None, "occ", "vir"), P(None, "occ", "vir"), P(None, ("occ", "vir")), P())
    return jax.shard_map(
        local, mesh=mesh, in_specs=placed, out_specs=P(None, ("occ", "vir"), None), check_vma=False
    )
```
